128 devices in a mesh: expert: 8 (over y, z_hi), mp: 16 (over x, z_lo, core).
Axes of the slice: x: 4, y: 4, z: 4 (z_hi: 2, z_lo: 2; z = z_hi * 2 + z_lo), core: 2. Of those that a mesh axis runs over, the one named last changes fastest.
Arguments:
- tokens: bfloat16 [8192, 4096], P(('expert', 'mp')), may hold values from -6 to 6
- attn_gain: float32 [4096], replicated, may hold values from 0.1 to 1.9
- query_weight: bfloat16 [4096, 4096], P(None, 'mp'), may hold values from -40 to 40
- key_weight: bfloat16 [4096, 1024], P(None, 'mp'), may hold values from -1 to 1
- value_weight: bfloat16 [4096, 1024], P(None, 'mp'), may hold values from -0.09375 to 0.09375
- output_weight: bfloat16 [4096, 4096], P('mp'), may hold values from -0.09375 to 0.09375
- ffn_gain: float32 [4096], replicated, may hold values from 0.1 to 1.9
- expert_gate: bfloat16 [8, 4096, 8192], P('expert', None, 'mp'), may hold values from -0.09375 to 0.09375
- expert_up: bfloat16 [8, 4096, 8192], P('expert', None, 'mp'), may hold values from -0.09375 to 0.09375
- expert_down: bfloat16 [8, 8192, 4096], P('expert', 'mp'), may hold values from -0.0625 to 0.0625
- expert_ids: int32 [8192, 2], P(('expert', 'mp')), may hold values from 0 to 7, all different within a row; in each aligned block of 64 rows (0 to 63, 64 to 127, ...) at most 24 rows name the same one
- route_weights: float32 [8192, 2], P(('expert', 'mp')), may hold values from 0.1 to 1
Outputs:
- attended: bfloat16 [8192, 4096], P(('expert', 'mp'))
- expert_mix: bfloat16 [8192, 4096], P(('expert', 'mp'))
The draws below stay inside these ranges and needn't reach their ends.
Inputs may be any that keep to these rules, and one draw needn't show every extreme that they name: `expert_ids`: each token names two different experts. Among the 64 tokens of one device (aligned blocks of rows) no expert is named more than 24 times, and in some blocks one is named exactly 24 times.
All inputs are finite; a program needn't handle non-finite values.
Results may differ from the reference program's by a relative error of at most 0.04.
Values may be sent and summed in bfloat16 or wider, within the bound.
No kernel may reach another device: no remote copies, remote signals or barrier semaphores. Data moves between devices by JAX's collectives and lax.ppermute only.
A program may use at most 192 MiB of HBM per device.

```python
import math
import jax
import jax.numpy as jnp
import numpy as np
from jax import lax

D = 4096
H = 32
KV = 8
HD = 128
FFW = 8192
TOK_DEV = 64
SEQ = 1024
TOKENS = 8192
EXPERTS = 8
CAP = 24
N_MP = 16


def shared_keys(key):
    bound = 6.0 / math.sqrt(D)
    base = jax.random.normal(key, (D, KV, HD), jnp.float32) / math.sqrt(D)
    return jnp.clip(base, -bound, bound)


def draw_key_weight(key, part):
    base = shared_keys(key)
    return base.reshape(D, KV * HD).astype(jnp.bfloat16)


def draw_query_weight(key, part):
    key = jax.random.fold_in(key, 12)
    noise = jnp.clip(jax.random.normal(key, (D, H, HD), jnp.float32), -6.0, 6.0) / math.sqrt(D)
    return noise.reshape(D, H * HD).astype(jnp.bfloat16)


def draw_tokens(key, part):
    key = jax.random.fold_in(key, 13)
    first_key = jax.random.fold_in(key, 0)
    return jnp.clip(jax.random.normal(first_key, (TOKENS, D), jnp.float32), -6.0, 6.0).astype(jnp.bfloat16)


def shard_levels(rng, extent, shards, least, top_value):
    level, own = 1.0, jax.random.fold_in(rng, 6)
    for position, blocks in shards:
        steps = jnp.exp(jax.random.uniform(jax.random.fold_in(own, position), (blocks,), jnp.float32, least / len(shards), top_value / len(shards)))
        level = level * jnp.repeat(steps, extent[position] // blocks).reshape([-1 if axis == position else 1 for axis in range(len(extent))])
    return level


def shared_out(own_key, own, number, rows, count, top, limit, slope):
    sequence = jax.random.permutation(own_key, count)
    heavy_load, usual = load_shares(count, rows * top, limit, slope, True), load_shares(count, rows * top, limit, slope, False)
    places = jnp.arange(count)

    def named(sizes, offset_by):
        used = int((sizes > 0).sum())
        fixed = max(1, used // 4)
        passed = fixed + (places - fixed + offset_by * (used - fixed)) % max(1, count - fixed)
        return jnp.zeros((count,), jnp.int32).at[sequence[jnp.where(places < fixed, places, passed)]].set(jnp.asarray(sizes, jnp.int32))

    sizes = jnp.where(number % 4 == 0, named(heavy_load, number // 4), named(usual, number - number // 4 - 1))
    mixed = jax.random.permutation(jax.random.fold_in(own, 3), count)
    giver, taker = mixed[0:count // 2 * 2:2], mixed[1:count // 2 * 2:2]
    margin = jnp.minimum(sizes[giver] - 1, limit - sizes[taker]) // 2
    margin = jnp.where((giver == sequence[0]) | (taker == sequence[0]) | (sizes[taker] == 0), 0, jnp.maximum(margin, 0))
    passed = jax.random.randint(jax.random.fold_in(own, 4), (count // 2,), 0, 1 << 20) % (margin + 1)
    sizes = sizes.at[giver].add(-passed).at[taker].add(passed)
    members = jnp.searchsorted(jnp.cumsum(sizes), jnp.arange(rows * top), side="right").astype(jnp.int32)
    grid = members.reshape(top, rows).T
    grid = grid[jax.random.permutation(jax.random.fold_in(own, 1), rows)]
    offset_by = jax.random.randint(jax.random.fold_in(own, 2), (rows, 1), 0, top)
    return jnp.take_along_axis(grid, (jnp.arange(top)[None, :] + offset_by) % top, axis=1)


def load_shares(count, total, reach, skew, full):
    portions = [(1 << 20) // math.isqrt(standing ** skew) + 1 for standing in range(1, count + 1)]
    largest = reach if full else min(reach, max(-(-total // count), total * portions[0] // sum(portions)))
    least = 1 if total - largest >= count - 1 else 0
    holding, surplus = [largest] + [least] * (count - 1), total - largest - least * (count - 1)
    while surplus > 0:
        free = [i for i in range(1, count) if holding[i] < largest] or [i for i in range(1, count) if holding[i] < reach]
        whole, remaining = sum([portions[i] for i in free]), surplus
        for i in free:
            addition = min(reach - holding[i], max(1, remaining * portions[i] // whole), surplus)
            holding[i] = holding[i] + addition
            surplus = surplus - addition
    return np.array(holding)


def bell_draw(stream_key, shape, deviation, most, pieces=(), kind=jnp.bfloat16):
    result = deviation * jax.random.normal(stream_key, shape, jnp.float32)
    if pieces:
        result = result * shard_levels(stream_key, shape, pieces, -0.22, 0.18)
    return jnp.clip(result, -most, most).astype(kind)


def setup_inputs(seed: int = 0) -> dict:
    seeds = jax.random.split(jax.random.key(seed), 13)
    tokens = draw_tokens(jax.random.fold_in(seeds[12], 71), 0)
    attn_gain = jnp.clip(1.0 + 0.18 * jax.random.normal(seeds[1], (D,), jnp.float32), 0.1, 1.9)
    query_weight = draw_query_weight(jax.random.fold_in(seeds[12], 71), 0)
    key_weight = draw_key_weight(jax.random.fold_in(seeds[12], 71), 0)
    value_weight = bell_draw(seeds[4], (D, KV * HD), D ** -0.5, 0.09375, ((1, 16),))
    output_weight = bell_draw(seeds[5], (H * HD, D), (H * HD) ** -0.5, 0.09375, ((0, 16),))
    ffn_gain = jnp.clip(1.0 + 0.18 * jax.random.normal(seeds[6], (D,), jnp.float32), 0.1, 1.9)
    expert_gate = bell_draw(seeds[7], (EXPERTS, D, FFW), D ** -0.5, 0.09375, ((0, 8), (2, 16)))
    expert_up = bell_draw(seeds[8], (EXPERTS, D, FFW), D ** -0.5, 0.09375, ((0, 8), (2, 16)))
    expert_down = bell_draw(seeds[9], (EXPERTS, FFW, D), FFW ** -0.5, 0.0625, ((0, 8), (1, 16)))
    expert_ids_keys = jax.random.split(jax.random.fold_in(seeds[10], 1), TOKENS // TOK_DEV)
    expert_ids_turns = jax.random.permutation(jax.random.fold_in(seeds[10], 3), TOKENS // TOK_DEV)
    expert_ids = jax.vmap(lambda own, number: shared_out(jax.random.fold_in(seeds[10], 2), own, number, TOK_DEV, EXPERTS, 2, CAP, 2))(expert_ids_keys, expert_ids_turns).reshape((TOKENS, 2))
    route_weights = jnp.clip(jnp.exp(math.log(1.0) - 2.3025851 * jax.random.uniform(seeds[11], (TOKENS, 2), jnp.float32) ** shard_levels(seeds[11], (TOKENS, 2), ((0, 128),), -0.2, 0.2)), 0.1, 1.0)
    return dict(tokens=tokens, attn_gain=attn_gain, query_weight=query_weight, key_weight=key_weight, value_weight=value_weight, output_weight=output_weight, ffn_gain=ffn_gain, expert_gate=expert_gate, expert_up=expert_up, expert_down=expert_down, expert_ids=expert_ids, route_weights=route_weights)


EPSILON = 1e-05
ROPE_BASE = 1000000.0

def rms_norm(inputs, gain):
    mean_square = lax.optimization_barrier(jnp.mean(inputs * inputs, axis=-1, keepdims=True))
    return inputs * lax.rsqrt(mean_square + EPSILON) * gain.astype(jnp.float32)

def rotate(columns, positions, offset):
    seq_len, width = columns.shape
    pair_index = (offset + 2 * jnp.arange(width // 2).astype(jnp.int32)) % HD // 2
    inverse_freq = jnp.power(ROPE_BASE, -2.0 * pair_index.astype(jnp.float32) / HD)
    angles = positions[:, None] * inverse_freq[None, :]
    cosine = jnp.cos(angles)
    sine = jnp.sin(angles)
    paired = columns.reshape(seq_len, width // 2, 2)
    first = paired[:, :, 0]
    second = paired[:, :, 1]
    turned = jnp.stack([first * cosine - second * sine, first * sine + second * cosine], axis=-1)
    return turned.reshape(seq_len, width)

def attend(query_block, key_block, value_block, score_scale):
    scores = jnp.einsum('qd,kd->qk', query_block, key_block, preferred_element_type=jnp.float32) * score_scale
    length = scores.shape[0]
    causal = jnp.arange(length)[:, None] >= jnp.arange(length)[None, :]
    scores = jnp.where(causal, scores, -1e+30)
    maxima = lax.optimization_barrier(jnp.max(scores, axis=-1, keepdims=True))
    expo = jnp.exp(scores - maxima)
    weights = (expo / lax.optimization_barrier(jnp.sum(expo, axis=-1, keepdims=True))).astype(jnp.bfloat16)
    return jnp.dot(weights, value_block, preferred_element_type=jnp.float32).astype(jnp.bfloat16)

def slot_table(ids_block, expert_count):
    flat_ids = ids_block.reshape(-1)
    onehot = (flat_ids[:, None] == jnp.arange(expert_count).astype(jnp.int32)[None, :]).astype(jnp.int32)
    earlier = jnp.cumsum(onehot, axis=0) - onehot
    return lax.optimization_barrier(jnp.sum(earlier * onehot, axis=1)).astype(jnp.int32)

def reference(tokens, attn_gain, query_weight, key_weight, value_weight, output_weight, ffn_gain, expert_gate, expert_up, expert_down, expert_ids, route_weights):
    inputs = tokens.astype(jnp.float32)
    normed = rms_norm(inputs, attn_gain).astype(jnp.bfloat16)
    positions = (jnp.arange(TOKENS) % SEQ).astype(jnp.float32)
    queries = rotate(jnp.dot(normed, query_weight, preferred_element_type=jnp.float32), positions, 0).astype(jnp.bfloat16)
    keys = rotate(jnp.dot(normed, key_weight, preferred_element_type=jnp.float32), positions, 0).astype(jnp.bfloat16)
    values = jnp.dot(normed, value_weight, preferred_element_type=jnp.float32).astype(jnp.bfloat16)
    n_seqs = TOKENS // SEQ
    seq_queries = queries.reshape(n_seqs, SEQ, H, HD)
    seq_keys = keys.reshape(n_seqs, SEQ, KV, HD)
    seq_values = values.reshape(n_seqs, SEQ, KV, HD)
    kv_of = (jnp.arange(H) // (H // KV)).astype(jnp.int32)
    score_scale = 1.0 / math.sqrt(HD)

    def one_sequence(blocks):
        block_q, block_k, block_v = blocks
        head_keys = jnp.take(block_k, kv_of, axis=1)
        head_values = jnp.take(block_v, kv_of, axis=1)
        return jax.vmap(attend, in_axes=(1, 1, 1, None), out_axes=1)(block_q, head_keys, head_values, score_scale)
    context = lax.map(one_sequence, (seq_queries, seq_keys, seq_values)).reshape(TOKENS, H * HD)
    group_cols = H * HD // N_MP
    attn_sum = jnp.zeros((TOKENS, D), jnp.float32)
    for group_index in range(N_MP):
        part_term = jnp.dot(context[:, group_index * group_cols:(group_index + 1) * group_cols], output_weight[group_index * group_cols:(group_index + 1) * group_cols], preferred_element_type=jnp.float32)
        attn_sum = attn_sum + lax.optimization_barrier(part_term.astype(jnp.bfloat16)).astype(jnp.float32)
    attended = (inputs + attn_sum).astype(jnp.bfloat16)
    normed_ffn = rms_norm(attended.astype(jnp.float32), ffn_gain).astype(jnp.bfloat16)
    devices = TOKENS // TOK_DEV
    id_blocks = expert_ids.reshape(devices, TOK_DEV, 2)
    slots = jax.vmap(slot_table, in_axes=(0, None))(id_blocks, EXPERTS)
    flat_ids = expert_ids.reshape(devices, 2 * TOK_DEV).astype(jnp.int32)
    device_index = jnp.arange(devices).astype(jnp.int32)[:, None]
    token_index = device_index * TOK_DEV + (jnp.arange(2 * TOK_DEV).astype(jnp.int32) // 2)[None, :]
    flat_pos = ((flat_ids * devices + device_index) * CAP + slots).astype(jnp.int32)
    table = jnp.full((EXPERTS * devices * CAP,), TOKENS, jnp.int32).at[flat_pos.reshape(-1)].set(token_index.reshape(-1).astype(jnp.int32))
    padded = jnp.concatenate([normed_ffn, jnp.zeros((1, D), jnp.bfloat16)], axis=0)
    hidden_cols = FFW // N_MP

    def run_expert(operands):
        table_row, gate_mat, up_mat, down_mat = operands
        rows = jnp.take(padded, table_row, axis=0)
        hidden = (jax.nn.silu(jnp.dot(rows, gate_mat, preferred_element_type=jnp.float32)) * jnp.dot(rows, up_mat, preferred_element_type=jnp.float32)).astype(jnp.bfloat16)
        total = jnp.zeros((rows.shape[0], D), jnp.float32)
        for shard_index in range(N_MP):
            part_term = jnp.dot(hidden[:, shard_index * hidden_cols:(shard_index + 1) * hidden_cols], down_mat[shard_index * hidden_cols:(shard_index + 1) * hidden_cols], preferred_element_type=jnp.float32)
            total = total + lax.optimization_barrier(part_term.astype(jnp.bfloat16)).astype(jnp.float32)
        return total.astype(jnp.bfloat16)
    outputs = lax.map(run_expert, (table.reshape(EXPERTS, devices * CAP), expert_gate, expert_up, expert_down))
    picked = jnp.take(outputs.reshape(-1, D), flat_pos.reshape(-1), axis=0).reshape(TOKENS, 2, D)
    expert_mix = lax.optimization_barrier(jnp.sum(picked.astype(jnp.float32) * route_weights[:, :, None], axis=1)).astype(jnp.bfloat16)
    return (attended, expert_mix)
```

```python
import math

import jax
import jax.numpy as jnp
import numpy as np
from jax import lax
from jax.experimental import pallas as pl
from jax.experimental.pallas import tpu as pltpu
from jax.sharding import PartitionSpec as P

D = 4096
HD = 128
EPSILON = 1e-05
ROPE_BASE = 1000000.0
VMEM_LIMIT = 56 * 1024 * 1024
LABELS = ((0, 0), (0, 1), (-1, 0), (1, 0), (-1, 1), (1, 1), (2, 0), (2, 1))


def to_z(i):
    return i ^ 2


def to_right(i):
    return (i + 4) % 16


def to_left(i):
    return (i + 12) % 16


def to_core(i):
    return i ^ 1


def send(value, lane0, lane1):
    pairs = [(i, lane1(i) if i % 2 else lane0(i)) for i in range(16)]
    return lax.ppermute(value, "mp", pairs)


def swap_cores(value):
    return send(value, to_core, to_core)


def gather_lane(own, first):
    from_z = send(own, to_z, to_z)
    from_left = send(own, to_right, to_right)
    from_right = send(own, to_left, to_left)
    left_z = send(jnp.where(first, from_z, from_left), to_right, to_z)
    right_z = send(jnp.where(first, from_z, from_right), to_left, to_z)
    across = send(jnp.where(first, from_left, from_right), to_right, to_left)
    across_z = send(jnp.where(first, left_z, across), to_right, to_z)
    return own, from_z, from_left, from_right, left_z, right_z, across, across_z


def add(base, *terms):
    total = base.astype(jnp.float32)
    for term in terms:
        total = total + term.astype(jnp.float32)
    return total


def only(flag, value):
    return jnp.where(flag, value, jnp.zeros_like(value))


def scatter_lane(parts, first):
    own, at_z, at_left, at_right, left_z, right_z, across, across_z = parts
    second = jnp.logical_not(first)
    low = lambda value: value.astype(jnp.bfloat16)
    r5 = send(left_z, to_left, to_z)
    r7 = send(across_z, to_right, to_z)
    r6 = send(low(add(across, only(second, r7))), to_right, to_left)
    r4 = send(low(add(right_z, only(first, r7))), to_right, to_z)
    r1 = send(low(add(at_z, only(first, r4), only(first, r5))), to_z, to_z)
    r2 = send(low(add(at_right, jnp.where(first, r6, r4))), to_right, to_right)
    r3 = send(low(add(at_left, only(second, r6), only(second, r5))), to_left, to_left)
    return add(own, r1, r2, r3)


def rms_norm(inputs, gain):
    mean_square = jnp.mean(inputs * inputs, axis=-1, keepdims=True)
    return inputs * lax.rsqrt(mean_square + EPSILON) * gain


def whole(shape):
    return pl.BlockSpec(shape, lambda *_: (0,) * len(shape))


def params():
    return pltpu.CompilerParams(vmem_limit_bytes=VMEM_LIMIT)


def project_kernel(count, *refs):
    blocks, weight, cosine, sine, out = refs[:count], *refs[count:]
    values_too = pl.program_id(0) == 2
    rows = blocks[0].shape[0]
    for number, block in enumerate(blocks):
        span = slice(number * rows, (number + 1) * rows)
        product = jnp.dot(block[...], weight[...], preferred_element_type=jnp.float32)
        even = lax.broadcasted_iota(jnp.int32, (rows, HD), 1) % 2 == 0
        for part in range(2):
            head = product[:, part * HD : (part + 1) * HD]
            swapped = jnp.where(even, pltpu.roll(head, HD - 1, 1), pltpu.roll(head, 1, 1))
            turned = head * cosine[span, :] + swapped * sine[span, :]
            if part == 1:
                turned = jnp.where(values_too, head, turned)
            out[span, part * HD : (part + 1) * HD] = turned.astype(jnp.bfloat16)


def project(blocks, weight, cosine, sine):
    rows = sum(block.shape[0] for block in blocks)
    width = weight.shape[1]
    return pl.pallas_call(
        lambda *refs: project_kernel(len(blocks), *refs),
        grid=(width // 256,),
        in_specs=[whole(block.shape) for block in blocks]
        + [pl.BlockSpec((D, 256), lambda j: (0, j)), whole((rows, HD)), whole((rows, HD))],
        out_specs=pl.BlockSpec((rows, 256), lambda j: (0, j)),
        out_shape=jax.ShapeDtypeStruct((rows, width), jnp.bfloat16),
        compiler_params=params(),
        cost_estimate=pl.CostEstimate(
            flops=2 * rows * D * width, bytes_accessed=2 * D * (rows + width), transcendentals=0
        ),
        name="project",
    )(*blocks, weight, cosine, sine)


def attend_kernel(qkv_a, qkv_b, other, pos_q, pos_k, out_own, out_other, *refs):
    outs, context = refs[:8], refs[8]
    half = qkv_a.shape[0]
    block = outs[0].shape[0]
    scale = 1.0 / math.sqrt(HD)
    for number, source in enumerate((qkv_a, qkv_b)):
        for tile in range(half // 128):
            rows = slice(tile * 128, (tile + 1) * 128)
            at = number * half + tile * 128
            allowed = pos_q[at : at + 128, :] >= pos_k[...]
            for head in range(4):
                query = source[rows, head * HD : (head + 1) * HD]
                scores = jnp.concatenate(
                    [
                        lax.dot_general(
                            query,
                            keys,
                            (((1,), (1,)), ((), ())),
                            preferred_element_type=jnp.float32,
                        )
                        for keys in (
                            qkv_a[:, 512:640],
                            qkv_b[:, 512:640],
                            other[:, 0:HD],
                        )
                    ],
                    axis=1,
                )
                scores = jnp.where(allowed, scores * scale, -1e30)
                maxima = jnp.max(scores, axis=-1, keepdims=True)
                expo = jnp.exp(scores - maxima)
                weights = (expo / jnp.sum(expo, axis=-1, keepdims=True)).astype(jnp.bfloat16)
                mixed = jnp.dot(
                    weights[:, :half], qkv_a[:, 640:768], preferred_element_type=jnp.float32
                )
                mixed += jnp.dot(
                    weights[:, half : 2 * half],
                    qkv_b[:, 640:768],
                    preferred_element_type=jnp.float32,
                )
                mixed += jnp.dot(
                    weights[:, 2 * half :], other[:, HD:], preferred_element_type=jnp.float32
                )
                context[at : at + 128, head * HD : (head + 1) * HD] = mixed.astype(jnp.bfloat16)
    for column in range(0, D, 512):
        cols = slice(column, column + 512)
        product = jnp.dot(
            context[:, :256], out_own[:, cols], preferred_element_type=jnp.float32
        ) + jnp.dot(context[:, 256:], out_other[:, cols], preferred_element_type=jnp.float32)
        for number, out in enumerate(outs):
            out[:, cols] = product[number * block : (number + 1) * block, :].astype(jnp.bfloat16)


def attend(qkv_a, qkv_b, other, pos_q, pos_k, out_own, out_other):
    rows = qkv_a.shape[0] + qkv_b.shape[0]
    block = rows // 8
    operands = (qkv_a, qkv_b, other, pos_q, pos_k, out_own, out_other)
    return pl.pallas_call(
        attend_kernel,
        in_specs=[whole(operand.shape) for operand in operands],
        out_specs=[whole((block, D))] * 8,
        out_shape=[jax.ShapeDtypeStruct((block, D), jnp.bfloat16)] * 8,
        scratch_shapes=[pltpu.VMEM((rows, 512), jnp.bfloat16)],
        compiler_params=params(),
        cost_estimate=pl.CostEstimate(
            flops=4 * rows * 512 * rows * 2 + 2 * rows * 512 * D,
            bytes_accessed=16 * 1024 * 1024,
            transcendentals=4 * rows * rows * 2,
        ),
        name="attend",
    )(*operands)


def expert_in_kernel(count, *refs):
    blocks = refs[:count]
    gates, ups, out = refs[count : count + 2], refs[count + 2 : count + 4], refs[count + 4]
    rows = blocks[0].shape[0]
    step = pl.program_id(0)

    def run(gate_ref, up_ref):
        for number, block in enumerate(blocks):
            gate = jnp.dot(block[...], gate_ref[...], preferred_element_type=jnp.float32)
            up = jnp.dot(block[...], up_ref[...], preferred_element_type=jnp.float32)
            hidden = gate / (1.0 + jnp.exp(-gate)) * up
            out[number * rows : (number + 1) * rows, :] = hidden.astype(jnp.bfloat16)

    @pl.when(step < 2)
    def _():
        run(gates[0], ups[0])

    @pl.when(step >= 2)
    def _():
        run(gates[1], ups[1])


def expert_in(blocks, gates, ups):
    block_rows = blocks[0].shape[0]
    rows = block_rows * len(blocks)
    own = pl.BlockSpec((D, 256), lambda j: (0, jnp.minimum(j, 1)))
    other = pl.BlockSpec((D, 256), lambda j: (0, jnp.maximum(j - 2, 0)))
    return pl.pallas_call(
        lambda *refs: expert_in_kernel(len(blocks), *refs),
        grid=(4,),
        in_specs=[whole(block.shape) for block in blocks] + [own, other, own, other],
        out_specs=pl.BlockSpec((rows, 256), lambda j: (0, j)),
        out_shape=jax.ShapeDtypeStruct((rows, 1024), jnp.bfloat16),
        compiler_params=params(),
        cost_estimate=pl.CostEstimate(
            flops=4 * rows * D * 1024,
            bytes_accessed=2 * D * (rows + 2048),
            transcendentals=rows * 1024,
        ),
        name="expert_in",
    )(*blocks, *gates, *ups)


def expert_out_kernel(count, hidden, down_own, down_other, *outs):
    rows = outs[0].shape[0]
    for number, out in enumerate(outs):
        span = slice(number * rows, (number + 1) * rows)
        product = jnp.dot(
            hidden[span, :512], down_own[...], preferred_element_type=jnp.float32
        ) + jnp.dot(hidden[span, 512:], down_other[...], preferred_element_type=jnp.float32)
        out[...] = product.astype(jnp.bfloat16)


def expert_out(hidden, downs, count):
    rows = hidden.shape[0]
    block = rows // count
    down = pl.BlockSpec((512, 512), lambda j: (0, j))
    return pl.pallas_call(
        lambda *refs: expert_out_kernel(count, *refs),
        grid=(D // 512,),
        in_specs=[whole(hidden.shape), down, down],
        out_specs=[pl.BlockSpec((block, 512), lambda j: (0, j))] * count,
        out_shape=[jax.ShapeDtypeStruct((block, D), jnp.bfloat16)] * count,
        compiler_params=params(),
        cost_estimate=pl.CostEstimate(
            flops=2 * rows * D * 1024,
            bytes_accessed=2 * D * (rows + 1024),
            transcendentals=0,
        ),
        name="expert_out",
    )(hidden, *downs)


def slot_table(ids_block, expert_count):
    flat_ids = ids_block.reshape(-1)
    onehot = (flat_ids[:, None] == jnp.arange(expert_count)[None, :]).astype(jnp.int32)
    earlier = jnp.cumsum(onehot, axis=0) - onehot
    return jnp.sum(earlier * onehot, axis=1)


def rope_tables():
    positions = np.arange(1024, dtype=np.float64)
    inverse = ROPE_BASE ** (-2.0 * np.arange(HD // 2) / HD)
    angles = np.repeat(positions[:, None] * inverse[None, :], 2, axis=1)
    sign = np.where(np.arange(HD) % 2 == 0, -1.0, 1.0)
    cosine = np.cos(angles).astype(np.float32).reshape(16, 64, HD)
    sine = (np.sin(angles) * sign).astype(np.float32).reshape(16, 64, HD)
    return cosine, sine


def on_device(
    tokens,
    attn_gain,
    query_weight,
    key_weight,
    value_weight,
    output_weight,
    ffn_gain,
    expert_gate,
    expert_up,
    expert_down,
    expert_ids,
    route_weights,
):
    expert_count = lax.axis_size("expert")
    rank = lax.axis_index("mp")
    core = rank % 2
    first = core == 0
    tok_rows = tokens.shape[0]
    inputs = tokens.astype(jnp.float32)
    normed = rms_norm(inputs, attn_gain).astype(jnp.bfloat16)

    kv_own = jnp.concatenate([key_weight, value_weight], axis=1)
    kv_other = swap_cores(kv_own)
    query_other = swap_cores(query_weight)
    output_other = swap_cores(output_weight)
    kv_low = jnp.where(first, kv_own, kv_other)
    kv_high = jnp.where(first, kv_other, kv_own)
    weight = jnp.concatenate(
        [query_weight, query_other, kv_low[:, :64], kv_high[:, :64], kv_low[:, 64:], kv_high[:, 64:]],
        axis=1,
    )

    blocks = gather_lane(normed, first)
    places = jnp.stack(
        [(rank // 4 + dx) % 4 * 4 + (rank // 2 % 2 ^ dz) * 2 for dx, dz in LABELS]
    )
    cosine_table, sine_table = rope_tables()
    lane_cosine = jnp.take(jnp.asarray(cosine_table), places + core, axis=0).reshape(-1, HD)
    lane_sine = jnp.take(jnp.asarray(sine_table), places + core, axis=0).reshape(-1, HD)
    offsets = jnp.arange(tok_rows)
    pos_own = ((places + core)[:, None] * tok_rows + offsets[None, :]).reshape(-1)
    pos_other = ((places + 1 - core)[:, None] * tok_rows + offsets[None, :]).reshape(-1)
    half = 4 * tok_rows
    qkv_a = project(blocks[:4], weight, lane_cosine[:half], lane_sine[:half])
    qkv_b = project(blocks[4:], weight, lane_cosine[half:], lane_sine[half:])
    kv_lane = jnp.concatenate([qkv_a[:, 512:], qkv_b[:, 512:]], axis=0)
    other = swap_cores(kv_lane)
    parts = attend(
        qkv_a,
        qkv_b,
        other,
        pos_own[:, None],
        jnp.concatenate([pos_own, pos_other])[None, :],
        output_weight,
        output_other,
    )
    attn_sum = scatter_lane(parts, first)
    attended = (inputs + attn_sum).astype(jnp.bfloat16)
    normed_ffn = rms_norm(attended.astype(jnp.float32), ffn_gain).astype(jnp.bfloat16)

    gate_own, up_own, down_own = expert_gate[0], expert_up[0], expert_down[0]
    gate_own, up_own, down_own, _ = lax.optimization_barrier(
        (gate_own, up_own, down_own, blocks[1])
    )
    gates = (gate_own, swap_cores(gate_own))
    ups = (up_own, swap_cores(up_own))
    downs = (down_own, swap_cores(down_own))

    capacity = 3 * tok_rows // expert_count
    slot_count = expert_count * capacity
    slots = slot_table(expert_ids, expert_count)
    targets = expert_ids.reshape(-1) * capacity + slots
    matches = (targets[:, None] == jnp.arange(slot_count)[None, :]).astype(jnp.bfloat16)
    matches = matches.reshape(tok_rows, 2, slot_count)
    dispatch_map = matches[:, 0] + matches[:, 1]
    outgoing = jnp.einsum(
        "tc,td->cd", dispatch_map, normed_ffn, preferred_element_type=jnp.float32
    ).astype(jnp.bfloat16)
    incoming = lax.all_to_all(
        outgoing.reshape(expert_count, capacity, D),
        "expert",
        split_axis=0,
        concat_axis=0,
        tiled=True,
    ).reshape(slot_count, D)

    rows = gather_lane(incoming, first)
    hidden_a = expert_in(rows[:4], gates, ups)
    hidden_b = expert_in(rows[4:7], gates, ups)
    hidden_c = expert_in(rows[7:], gates, ups)
    parts = (
        list(expert_out(hidden_a, downs, 4))
        + list(expert_out(hidden_b, downs, 3))
        + list(expert_out(hidden_c, downs, 1))
    )
    summed = scatter_lane(parts, first).astype(jnp.bfloat16)
    returned = lax.all_to_all(
        summed.reshape(expert_count, capacity, D), "expert", split_axis=0, concat_axis=0, tiled=True
    )
    picked = jnp.einsum(
        "tkc,cd->tkd", matches, returned.reshape(slot_count, D), preferred_element_type=jnp.float32
    )
    expert_mix = jnp.sum(picked * route_weights[:, :, None], axis=1).astype(jnp.bfloat16)
    return (attended, expert_mix)


def solution(mesh):
    in_specs = (
        P(("expert", "mp"), None),
        P(),
        P(None, "mp"),
        P(None, "mp"),
        P(None, "mp"),
        P("mp", None),
        P(),
        P("expert", None, "mp"),
        P("expert", None, "mp"),
        P("expert", "mp", None),
        P(("expert", "mp"), None),
        P(("expert", "mp"), None),
    )
    out_specs = (P(("expert", "mp"), None), P(("expert", "mp"), None))
    return jax.shard_map(
        on_device, mesh=mesh, in_specs=in_specs, out_specs=out_specs, check_vma=False
    )
```

```python
import math

import jax
import jax.numpy as jnp
import numpy as np
from jax import lax
from jax.experimental import pallas as pl
from jax.experimental.pallas import tpu as pltpu
from jax.sharding import PartitionSpec as P

D = 4096
HD = 128
EPSILON = 1e-05
ROPE_BASE = 1000000.0
LABELS = (
    ((0, 0), (0, 1), (-1, 0), (1, 0), (1, 1), (-1, 1), (2, 0), (2, 1)),
    ((0, 0), (-1, 0), (0, 1), (1, 0), (2, 0), (-1, 1), (1, 1), (2, 1)),
)


def to_z(i):
    return i ^ 2


def to_right(i):
    return (i + 4) % 16


def to_left(i):
    return (i + 12) % 16


def to_core(i):
    return i ^ 1


def send(value, lane0, lane1):
    pairs = [(i, lane1(i) if i % 2 else lane0(i)) for i in range(16)]
    return lax.ppermute(value, "mp", pairs)


def swap_cores(value):
    return send(value, to_core, to_core)


def gather_lane(own):
    a = send(own, to_z, to_right)
    c = send(own, to_left, to_left)
    b = send(own, to_right, to_z)
    s = send(a, to_left, to_right)
    r5 = send(a, to_right, to_z)
    s1 = send(c, to_left, to_z)
    r7 = send(s, to_left, to_z)
    return own, a, b, c, s, r5, s1, r7


def add(base, *terms):
    total = base.astype(jnp.float32)
    for term in terms:
        total = total + term.astype(jnp.float32)
    return total


def scatter_lane(parts):
    own, a, b, c, s, r5, s1, r7 = parts
    low = lambda value: value.astype(jnp.bfloat16)
    b_in = send(b, to_left, to_z)
    r5_in = send(r5, to_left, to_z)
    s1_in = send(s1, to_right, to_z)
    c_in = send(low(add(c, s1_in)), to_right, to_right)
    r7_in = send(r7, to_right, to_z)
    s_in = send(low(add(s, r7_in)), to_right, to_left)
    a_in = send(low(add(a, s_in, r5_in)), to_z, to_left)
    return add(own, b_in, c_in, a_in)


def rms_norm(inputs, gain):
    mean_square = jnp.mean(inputs * inputs, axis=-1, keepdims=True)
    return inputs * lax.rsqrt(mean_square + EPSILON) * gain


def params(mebibytes):
    return pltpu.CompilerParams(vmem_limit_bytes=mebibytes * 1024 * 1024)


ANY = pl.BlockSpec(memory_space=pl.ANY)
SMEM = pl.BlockSpec(memory_space=pltpu.SMEM)
VMEM = pl.BlockSpec(memory_space=pltpu.VMEM)


def stack(refs):
    return jnp.concatenate([ref[...] for ref in refs], axis=0)


def project_kernel(count, core, *refs):
    blocks, weights, (cosine, sine, out) = refs[:count], refs[count : count + 4], refs[count + 4 :]
    rows = cosine.shape[0]
    lane = lax.broadcasted_iota(jnp.int32, (rows, HD), 1)

    def turn(head):
        swapped = jnp.where(lane % 2 == 0, pltpu.roll(head, HD - 1, 1), pltpu.roll(head, 1, 1))
        return (head * cosine[...] + swapped * sine[...]).astype(jnp.bfloat16)

    for number in range(2):
        product = jnp.dot(stack(blocks), weights[number][...], preferred_element_type=jnp.float32)
        for part in range(2):
            at = number * 256 + part * HD
            out[:, at : at + HD] = turn(product[:, part * HD : (part + 1) * HD])
    pair = jnp.concatenate([weights[2][...], weights[3][...]], axis=1)
    product = jnp.dot(stack(blocks), pair, preferred_element_type=jnp.float32)
    own, other = product[:, :HD], product[:, HD:]
    first = core[0] == 0
    low = jnp.where(first, own, other)
    high = jnp.where(first, other, own)
    below = lane < HD // 2
    out[:, 512:640] = turn(jnp.where(below, low, pltpu.roll(high, HD // 2, 1)))
    out[:, 640:768] = jnp.where(below, pltpu.roll(low, HD // 2, 1), high).astype(jnp.bfloat16)


def project(blocks, weights, core, cosine, sine):
    count = len(blocks)
    rows = sum(block.shape[0] for block in blocks)
    return pl.pallas_call(
        lambda *refs: project_kernel(count, *refs),
        in_specs=[SMEM] + [VMEM] * (count + 6),
        out_specs=VMEM,
        out_shape=jax.ShapeDtypeStruct((rows, 768), jnp.bfloat16),
        compiler_params=params(20),
        cost_estimate=pl.CostEstimate(
            flops=2 * rows * D * 768, bytes_accessed=2 * D * (rows + 768), transcendentals=0
        ),
        name="project",
    )(core, *blocks, *weights, cosine, sine)


def attend_kernel(bases, qkv_a, qkv_b, other, pos_k, out_own, out_other, *refs):
    outs = refs[:8]
    keys, values, scores, weights, context, result, out_sems = refs[8:]
    half = qkv_a.shape[0]
    rows = 2 * half
    block = outs[0].shape[0]
    for number, source in enumerate((qkv_a, qkv_b)):
        span = slice(number * half, (number + 1) * half)
        keys[span, :] = source[:, 512:640]
        values[span, :] = source[:, 640:768]
    keys[rows:, :] = other[:, :HD]
    values[rows:, :] = other[:, HD:]
    scale = math.log2(math.e) / math.sqrt(HD)
    tiles = rows // 128
    out_copies = []
    for tile in range(tiles):
        slot = tile % 2
        source = (qkv_a, qkv_b)[tile * 128 // half]
        at = tile * 128 % half
        queries = jnp.concatenate(
            [source[at : at + 128, head * HD : (head + 1) * HD] for head in range(4)], axis=0
        )
        scores[slot] = lax.dot_general(
            queries, keys[...], (((1,), (1,)), ((), ())), preferred_element_type=jnp.float32
        )
        sums = []
        for piece in range(8):
            start = piece * 64
            pos_q = bases[2 * tile + piece % 2] + lax.broadcasted_iota(jnp.int32, (64, 1), 0)
            masked = jnp.where(pos_q >= pos_k[...], scores[slot, start : start + 64, :], -1e30)
            maxima = jnp.max(masked, axis=-1, keepdims=True)
            expo = jnp.exp2(masked * scale - maxima * scale)
            sums.append(jnp.sum(expo, axis=-1, keepdims=True))
            weights[slot, start : start + 64, :] = expo.astype(jnp.bfloat16)
        mixed = jnp.dot(weights[slot], values[...], preferred_element_type=jnp.float32)
        mixed = (mixed / jnp.concatenate(sums, axis=0)).astype(jnp.bfloat16)
        for head in range(4):
            context[tile * 128 : (tile + 1) * 128, head * HD : (head + 1) * HD] = mixed[
                head * 128 : (head + 1) * 128, :
            ]
        if tile % 2:
            pair = slice((tile - 1) * 128, (tile + 1) * 128)
            for column in range(0, D, 1024):
                cols = slice(column, column + 1024)
                product = jnp.dot(
                    context[pair, :256], out_own[:, cols], preferred_element_type=jnp.float32
                ) + jnp.dot(
                    context[pair, 256:], out_other[:, cols], preferred_element_type=jnp.float32
                )
                result[pair, cols] = product.astype(jnp.bfloat16)
            for number in range((tile - 1) * 128 // block, (tile + 1) * 128 // block):
                copy = pltpu.make_async_copy(
                    result.at[pl.ds(number * block, block), :], outs[number], out_sems.at[number]
                )
                copy.start()
                out_copies.append(copy)
    for copy in out_copies:
        copy.wait()


def attend(bases, qkv_a, qkv_b, other, pos_k, out_own, out_other):
    rows = qkv_a.shape[0] + qkv_b.shape[0]
    block = rows // 8
    operands = (qkv_a, qkv_b, other, pos_k)
    return pl.pallas_call(
        attend_kernel,
        in_specs=[SMEM] + [VMEM] * 6,
        out_specs=[ANY] * 8,
        out_shape=[jax.ShapeDtypeStruct((block, D), jnp.bfloat16)] * 8,
        scratch_shapes=[
            pltpu.VMEM((2 * rows, HD), jnp.bfloat16),
            pltpu.VMEM((2 * rows, HD), jnp.bfloat16),
            pltpu.VMEM((2, 512, 2 * rows), jnp.float32),
            pltpu.VMEM((2, 512, 2 * rows), jnp.bfloat16),
            pltpu.VMEM((rows, 512), jnp.bfloat16),
            pltpu.VMEM((rows, D), jnp.bfloat16),
            pltpu.SemaphoreType.DMA((8,)),
        ],
        compiler_params=params(28),
        cost_estimate=pl.CostEstimate(
            flops=4 * rows * 512 * rows * 2 + 2 * rows * 512 * D,
            bytes_accessed=16 * 1024 * 1024,
            transcendentals=4 * rows * rows * 2,
        ),
        name="attend",
    )(bases, *operands, out_own, out_other)


def expert_in_kernel(count, *refs):
    blocks, weights, out = refs[:count], refs[count : count + 4], refs[count + 4]
    for part in range(2):
        for column in (0, 256):
            cols = slice(column, column + 256)
            gate = jnp.dot(stack(blocks), weights[part][:, cols], preferred_element_type=jnp.float32)
            up = jnp.dot(
                stack(blocks), weights[2 + part][:, cols], preferred_element_type=jnp.float32
            )
            hidden = gate / (1.0 + jnp.exp(-gate)) * up
            at = part * 512 + column
            out[:, at : at + 256] = hidden.astype(jnp.bfloat16)


def expert_in(blocks, gates, ups):
    rows = sum(block.shape[0] for block in blocks)
    return pl.pallas_call(
        lambda *refs: expert_in_kernel(len(blocks), *refs),
        in_specs=[VMEM] * (len(blocks) + 4),
        out_specs=VMEM,
        out_shape=jax.ShapeDtypeStruct((rows, 1024), jnp.bfloat16),
        compiler_params=params(28),
        cost_estimate=pl.CostEstimate(
            flops=4 * rows * D * 1024,
            bytes_accessed=2 * D * (rows + 2048),
            transcendentals=rows * 1024,
        ),
        name="expert_in",
    )(*blocks, *gates, *ups)


def expert_out_kernel(hidden, down_own, down_other, *outs):
    rows = outs[0].shape[0]
    for column in range(0, D, 512):
        cols = slice(column, column + 512)
        product = jnp.dot(
            hidden[:, :512], down_own[:, cols], preferred_element_type=jnp.float32
        ) + jnp.dot(hidden[:, 512:], down_other[:, cols], preferred_element_type=jnp.float32)
        for number, out in enumerate(outs):
            out[:, cols] = product[number * rows : (number + 1) * rows, :].astype(jnp.bfloat16)


def expert_out(hidden, downs, count):
    rows = hidden.shape[0]
    return pl.pallas_call(
        expert_out_kernel,
        in_specs=[VMEM] * 3,
        out_specs=[VMEM] * count,
        out_shape=[jax.ShapeDtypeStruct((rows // count, D), jnp.bfloat16)] * count,
        compiler_params=params(20),
        cost_estimate=pl.CostEstimate(
            flops=2 * rows * D * 1024,
            bytes_accessed=2 * D * (rows + 1024) + 2048 * rows,
            transcendentals=0,
        ),
        name="expert_out",
    )(hidden, *downs)


def slot_table(ids_block, expert_count):
    flat_ids = ids_block.reshape(-1)
    onehot = (flat_ids[:, None] == jnp.arange(expert_count)[None, :]).astype(jnp.int32)
    earlier = jnp.cumsum(onehot, axis=0) - onehot
    return jnp.sum(earlier * onehot, axis=1)


def rope_tables():
    positions = np.arange(1024, dtype=np.float64)
    inverse = ROPE_BASE ** (-2.0 * np.arange(HD // 2) / HD)
    angles = np.repeat(positions[:, None] * inverse[None, :], 2, axis=1)
    sign = np.where(np.arange(HD) % 2 == 0, -1.0, 1.0)
    cosine = np.cos(angles).astype(np.float32).reshape(16, 64, HD)
    sine = (np.sin(angles) * sign).astype(np.float32).reshape(16, 64, HD)
    return cosine, sine


def on_device(
    tokens,
    attn_gain,
    query_weight,
    key_weight,
    value_weight,
    output_weight,
    ffn_gain,
    expert_gate,
    expert_up,
    expert_down,
    expert_ids,
    route_weights,
):
    expert_count = lax.axis_size("expert")
    rank = lax.axis_index("mp")
    core = rank % 2
    first = core == 0
    tok_rows = tokens.shape[0]
    inputs = tokens.astype(jnp.float32)
    normed = rms_norm(inputs, attn_gain).astype(jnp.bfloat16)

    blocks = gather_lane(normed)
    kv_own = jnp.concatenate([key_weight, value_weight], axis=1)
    kv_other = swap_cores(kv_own)
    query_other = swap_cores(query_weight)
    output_other = swap_cores(output_weight)
    places = jnp.stack(
        [
            jnp.where(
                first,
                *((rank // 4 + dx) % 4 * 4 + (rank // 2 % 2 ^ dz) * 2 for dx, dz in pair),
            )
            for pair in zip(*LABELS)
        ]
    )
    other_places = jnp.stack(
        [
            jnp.where(
                first,
                *((rank // 4 + dx) % 4 * 4 + (rank // 2 % 2 ^ dz) * 2 for dx, dz in pair[::-1]),
            )
            for pair in zip(*LABELS)
        ]
    )
    cosine_table, sine_table = rope_tables()
    lane_cosine = jnp.take(jnp.asarray(cosine_table), places + core, axis=0).reshape(-1, HD)
    lane_sine = jnp.take(jnp.asarray(sine_table), places + core, axis=0).reshape(-1, HD)
    offsets = jnp.arange(tok_rows)
    bases = ((places + core) * tok_rows).astype(jnp.int32)
    pos_own = (bases[:, None] + offsets[None, :]).reshape(-1)
    pos_other = ((other_places + 1 - core)[:, None] * tok_rows + offsets[None, :]).reshape(-1)
    half = 4 * tok_rows
    weights = (query_weight, query_other, kv_own, kv_other)
    core_flag = core.astype(jnp.int32).reshape(1)
    qkv_a = project(blocks[:4], weights, core_flag, lane_cosine[:half], lane_sine[:half])
    late, qkv_a = lax.optimization_barrier((blocks[4:], qkv_a))
    qkv_b = project(late, weights, core_flag, lane_cosine[half:], lane_sine[half:])
    kv_lane = jnp.concatenate([qkv_a[:, 512:], qkv_b[:, 512:]], axis=0)
    other = swap_cores(kv_lane)
    parts = attend(
        bases,
        qkv_a,
        qkv_b,
        other,
        jnp.concatenate([pos_own, pos_other]).astype(jnp.int32)[None, :],
        output_weight,
        output_other,
    )
    attn_sum = scatter_lane(parts)
    attended = (inputs + attn_sum).astype(jnp.bfloat16)
    normed_ffn = rms_norm(attended.astype(jnp.float32), ffn_gain).astype(jnp.bfloat16)

    gate_own, up_own, down_own = expert_gate[0], expert_up[0], expert_down[0]
    gate_own, up_own, down_own, _ = lax.optimization_barrier(
        (gate_own, up_own, down_own, blocks[1])
    )
    gates = (gate_own, swap_cores(gate_own))
    ups = (up_own, swap_cores(up_own))
    downs = (down_own, swap_cores(down_own))

    capacity = 3 * tok_rows // expert_count
    slot_count = expert_count * capacity
    slots = slot_table(expert_ids, expert_count)
    targets = expert_ids.reshape(-1) * capacity + slots
    matches = (targets[:, None] == jnp.arange(slot_count)[None, :]).astype(jnp.bfloat16)
    matches = matches.reshape(tok_rows, 2, slot_count)
    dispatch_map = matches[:, 0] + matches[:, 1]

    def exchange(value, width):
        value = value.reshape(expert_count, width, D)
        value = lax.all_to_all(value, "expert", split_axis=0, concat_axis=0, tiled=True)
        return value.reshape(expert_count * width, D)

    def take_slots(value, span):
        shape = value.shape[:-1]
        value = value.reshape(*shape, expert_count, capacity)[..., span]
        return value.reshape(*shape, -1)

    total = 0.0
    for span in (slice(0, 16), slice(16, 24)):
        width = span.stop - span.start
        outgoing = jnp.einsum(
            "tc,td->cd",
            take_slots(dispatch_map, span),
            normed_ffn,
            preferred_element_type=jnp.float32,
        ).astype(jnp.bfloat16)
        rows = gather_lane(exchange(outgoing, width))
        hidden_a = expert_in(rows[:4], gates, ups)
        parts_a = expert_out(hidden_a, downs, 4)
        hidden_a, late = lax.optimization_barrier((hidden_a, rows[4:7]))
        hidden_b = expert_in(late, gates, ups)
        parts_b = expert_out(hidden_b, downs, 3)
        hidden_b, late = lax.optimization_barrier((hidden_b, rows[7:]))
        hidden_c = expert_in(late, gates, ups)
        parts_c = expert_out(hidden_c, downs, 1)
        summed = scatter_lane([*parts_a, *parts_b, *parts_c]).astype(jnp.bfloat16)
        picked = jnp.einsum(
            "tkc,cd->tkd",
            take_slots(matches, span),
            exchange(summed, width),
            preferred_element_type=jnp.float32,
        )
        total += jnp.sum(picked * route_weights[:, :, None], axis=1)
    expert_mix = total.astype(jnp.bfloat16)
    return (attended, expert_mix)


def solution(mesh):
    in_specs = (
        P(("expert", "mp"), None),
        P(),
        P(None, "mp"),
        P(None, "mp"),
        P(None, "mp"),
        P("mp", None),
        P(),
        P("expert", None, "mp"),
        P("expert", None, "mp"),
        P("expert", "mp", None),
        P(("expert", "mp"), None),
        P(("expert", "mp"), None),
    )
    out_specs = (P(("expert", "mp"), None), P(("expert", "mp"), None))
    return jax.shard_map(
        on_device, mesh=mesh, in_specs=in_specs, out_specs=out_specs, check_vma=False
    )
```

```python
import math

import jax
import jax.numpy as jnp
import numpy as np
from jax import lax
from jax.experimental import pallas as pl
from jax.experimental.pallas import tpu as pltpu
from jax.sharding import PartitionSpec as P

D = 4096
HD = 128
EPSILON = 1e-05
ROPE_BASE = 1000000.0
SHARE = 0.4
LABELS = (
    ((0, 0), (0, 1), (-1, 0), (1, 0), (1, 1), (-1, 1), (2, 0), (2, 1)),
    ((0, 0), (-1, 0), (0, 1), (1, 0), (2, 0), (-1, 1), (1, 1), (2, 1)),
)


def to_z(i):
    return i ^ 2


def to_right(i):
    return (i + 4) % 16


def to_left(i):
    return (i + 12) % 16


def to_core(i):
    return i ^ 1


def send(value, lane0, lane1):
    pairs = [(i, lane1(i) if i % 2 else lane0(i)) for i in range(16)]
    return lax.ppermute(value, "mp", pairs)


def swap_cores(value):
    return send(value, to_core, to_core)


def sides(mirrored):
    return (to_right, to_left) if mirrored else (to_left, to_right)


def gather_lane(own, mirrored=False):
    left, right = sides(mirrored)
    a = send(own, to_z, right)
    c = send(own, left, left)
    b = send(own, right, to_z)
    s = send(a, left, right)
    r5 = send(a, right, to_z)
    s1 = send(c, left, to_z)
    return [own, a, b, c, s, r5, s1]


def gather_last(s, mirrored=False):
    left, _ = sides(mirrored)
    return send(s, left, to_z)


def tie(value, *others):
    return pl.pallas_call(
        lambda *refs: None,
        in_specs=[ANY] * (1 + len(others)),
        out_specs=ANY,
        out_shape=jax.ShapeDtypeStruct(value.shape, value.dtype),
        input_output_aliases={0: 0},
        compiler_params=params(1),
        cost_estimate=cost(0, 0),
        name="tie",
    )(value, *others)


def add(base, *terms):
    total = base.astype(jnp.float32)
    for term in terms:
        total = total + term.astype(jnp.float32)
    return total


def scatter_lane(parts, mirrored=False, swapped=False):
    own, a, b, c, s, r5, s1, r7 = parts
    left, right = sides(mirrored)
    low = lambda value: value.astype(jnp.bfloat16)
    if swapped:
        a, b, s, s1 = b, a, s1, s

    def give(value, lane0, lane1):
        return send(value, lane1, lane0) if swapped else send(value, lane0, lane1)

    r5_in = give(r5, left, to_z)
    s1_in = give(s1, right, to_z)
    r7_in = give(r7, right, to_z)
    c_in = give(low(add(c, s1_in)), right, right)
    s_in = give(low(add(s, r7_in)), right, left)
    b_in = give(tie(b, r7_in, s1_in), left, to_z)
    a_in = give(low(add(a, s_in, r5_in)), to_z, left)
    return add(own, b_in, c_in, a_in)


def rms_norm(inputs, gain):
    mean_square = jnp.mean(inputs * inputs, axis=-1, keepdims=True)
    return inputs * lax.rsqrt(mean_square + EPSILON) * gain


def cost(flops, bytes_accessed, transcendentals=0):
    return pl.CostEstimate(
        flops=int(SHARE * flops),
        bytes_accessed=int(SHARE * bytes_accessed),
        transcendentals=int(SHARE * transcendentals),
    )


def params(mebibytes):
    return pltpu.CompilerParams(vmem_limit_bytes=mebibytes * 1024 * 1024)


ANY = pl.BlockSpec(memory_space=pl.ANY)
SMEM = pl.BlockSpec(memory_space=pltpu.SMEM)
VMEM = pl.BlockSpec(memory_space=pltpu.VMEM)
HBM = pl.BlockSpec(memory_space=pltpu.HBM)


def stack(refs):
    return jnp.concatenate([ref[...] for ref in refs], axis=0)


def stage_kernel(count, *refs):
    sources, targets, token, sems = refs[:count], refs[-2 - count : -2], refs[-2], refs[-1]
    copies = [
        pltpu.make_async_copy(source, target, sems.at[number])
        for number, (source, target) in enumerate(zip(sources, targets))
    ]
    for copy in copies:
        copy.start()
    token[...] = jnp.zeros_like(token)
    for copy in copies:
        copy.wait()


def stage(arrays, after):
    count = len(arrays)
    token = jax.ShapeDtypeStruct((8, HD), jnp.float32)
    return pl.pallas_call(
        lambda *refs: stage_kernel(count, *refs),
        in_specs=[HBM] * count + [ANY] * len(after),
        out_specs=[VMEM] * (count + 1),
        out_shape=[jax.ShapeDtypeStruct(array.shape, array.dtype) for array in arrays] + [token],
        scratch_shapes=[pltpu.SemaphoreType.DMA((count,))],
        compiler_params=params(28),
        cost_estimate=cost(0, 2 * sum(array.size for array in arrays)),
        name="stage",
    )(*arrays, *after)


def project_kernel(count, places, *refs):
    blocks, weights, tables = refs[:count], refs[count : count + 4], refs[count + 4 : count + 6]
    out = refs[-1]
    rows = out.shape[0]
    cosine, sine = (
        jnp.concatenate([table[places[number]] for number in range(count)], axis=0)
        for table in tables
    )
    lane = lax.broadcasted_iota(jnp.int32, (rows, HD), 1)

    def turn(head):
        swapped = jnp.where(lane % 2 == 0, pltpu.roll(head, HD - 1, 1), pltpu.roll(head, 1, 1))
        return (head * cosine + swapped * sine).astype(jnp.bfloat16)

    for number in range(2):
        product = jnp.dot(stack(blocks), weights[number][...], preferred_element_type=jnp.float32)
        for part in range(2):
            at = number * 256 + part * HD
            out[:, at : at + HD] = turn(product[:, part * HD : (part + 1) * HD])
    pair = jnp.concatenate([weights[2][...], weights[3][...]], axis=1)
    product = jnp.dot(stack(blocks), pair, preferred_element_type=jnp.float32)
    own, other = product[:, :HD], product[:, HD:]
    first = places[0] % 2 == 0
    low = jnp.where(first, own, other)
    high = jnp.where(first, other, own)
    below = lane < HD // 2
    out[:, 512:640] = turn(jnp.where(below, low, pltpu.roll(high, HD // 2, 1)))
    out[:, 640:768] = jnp.where(below, pltpu.roll(low, HD // 2, 1), high).astype(jnp.bfloat16)


def project(blocks, weights, places, cosine, sine, after=()):
    count = len(blocks)
    rows = sum(block.shape[0] for block in blocks)
    return pl.pallas_call(
        lambda *refs: project_kernel(count, *refs),
        in_specs=[SMEM] + [VMEM] * (count + 6) + [ANY] * len(after),
        out_specs=VMEM,
        out_shape=jax.ShapeDtypeStruct((rows, 768), jnp.bfloat16),
        compiler_params=params(20),
        cost_estimate=cost(
            2 * rows * D * 768, 2 * D * (rows + 768), 0
        ),
        name="project",
    )(places, *blocks, *weights, cosine, sine, *after)


def attend_kernel(bases, qkv_a, qkv_b, other, pos_k, out_own, out_other, *refs):
    outs = refs[:8]
    keys, values, scores, weights, context, result, out_sems = refs[8:]
    half = qkv_a.shape[0]
    rows = 2 * half
    block = outs[0].shape[0]
    for number, source in enumerate((qkv_a, qkv_b)):
        span = slice(number * half, (number + 1) * half)
        keys[span, :] = source[:, 512:640]
        values[span, :] = source[:, 640:768]
    keys[rows:, :] = other[:, :HD]
    values[rows:, :] = other[:, HD:]
    scale = math.log2(math.e) / math.sqrt(HD)
    tiles = rows // 128
    out_copies = []
    for tile in range(tiles):
        slot = tile % 2
        source = (qkv_a, qkv_b)[tile * 128 // half]
        at = tile * 128 % half
        queries = jnp.concatenate(
            [source[at : at + 128, head * HD : (head + 1) * HD] for head in range(4)], axis=0
        )
        scores[slot] = lax.dot_general(
            queries, keys[...], (((1,), (1,)), ((), ())), preferred_element_type=jnp.float32
        )
        sums = []
        for piece in range(8):
            start = piece * 64
            pos_q = bases[2 * tile + piece % 2] + lax.broadcasted_iota(jnp.int32, (64, 1), 0)
            masked = jnp.where(pos_q >= pos_k[...], scores[slot, start : start + 64, :], -1e30)
            maxima = jnp.max(masked, axis=-1, keepdims=True)
            expo = jnp.exp2(masked * scale - maxima * scale)
            sums.append(jnp.sum(expo, axis=-1, keepdims=True))
            weights[slot, start : start + 64, :] = expo.astype(jnp.bfloat16)
        mixed = jnp.dot(weights[slot], values[...], preferred_element_type=jnp.float32)
        mixed = (mixed / jnp.concatenate(sums, axis=0)).astype(jnp.bfloat16)
        for head in range(4):
            context[tile * 128 : (tile + 1) * 128, head * HD : (head + 1) * HD] = mixed[
                head * 128 : (head + 1) * 128, :
            ]
        if tile % 2:
            pair = slice((tile - 1) * 128, (tile + 1) * 128)
            for column in range(0, D, 1024):
                cols = slice(column, column + 1024)
                product = jnp.dot(
                    context[pair, :256], out_own[:, cols], preferred_element_type=jnp.float32
                ) + jnp.dot(
                    context[pair, 256:], out_other[:, cols], preferred_element_type=jnp.float32
                )
                result[pair, cols] = product.astype(jnp.bfloat16)
            for number in range((tile - 1) * 128 // block, (tile + 1) * 128 // block):
                copy = pltpu.make_async_copy(
                    result.at[pl.ds(number * block, block), :], outs[number], out_sems.at[number]
                )
                copy.start()
                out_copies.append(copy)
    for copy in out_copies:
        copy.wait()


def attend(bases, qkv_a, qkv_b, other, pos_k, out_own, out_other):
    rows = qkv_a.shape[0] + qkv_b.shape[0]
    block = rows // 8
    operands = (qkv_a, qkv_b, other, pos_k)
    return pl.pallas_call(
        attend_kernel,
        in_specs=[SMEM] + [VMEM] * 6,
        out_specs=[ANY] * 8,
        out_shape=[jax.ShapeDtypeStruct((block, D), jnp.bfloat16)] * 8,
        scratch_shapes=[
            pltpu.VMEM((2 * rows, HD), jnp.bfloat16),
            pltpu.VMEM((2 * rows, HD), jnp.bfloat16),
            pltpu.VMEM((2, 512, 2 * rows), jnp.float32),
            pltpu.VMEM((2, 512, 2 * rows), jnp.bfloat16),
            pltpu.VMEM((rows, 512), jnp.bfloat16),
            pltpu.VMEM((rows, D), jnp.bfloat16),
            pltpu.SemaphoreType.DMA((8,)),
        ],
        compiler_params=params(28),
        cost_estimate=cost(
            4 * rows * 512 * rows * 2 + 2 * rows * 512 * D,
            16 * 1024 * 1024,
            4 * rows * rows * 2,
        ),
        name="attend",
    )(bases, *operands, out_own, out_other)


def expert_in_kernel(count, *refs):
    blocks, weights, out = refs[:count], refs[count : count + 4], refs[-1]
    for part in range(2):
        for column in (0, 256):
            cols = slice(column, column + 256)
            gate = jnp.dot(stack(blocks), weights[part][:, cols], preferred_element_type=jnp.float32)
            up = jnp.dot(
                stack(blocks), weights[2 + part][:, cols], preferred_element_type=jnp.float32
            )
            hidden = gate / (1.0 + jnp.exp(-gate)) * up
            at = part * 512 + column
            out[:, at : at + 256] = hidden.astype(jnp.bfloat16)


def expert_in(blocks, gates, ups, after=()):
    rows = sum(block.shape[0] for block in blocks)
    return pl.pallas_call(
        lambda *refs: expert_in_kernel(len(blocks), *refs),
        in_specs=[VMEM] * (len(blocks) + 4) + [ANY] * len(after),
        out_specs=VMEM,
        out_shape=jax.ShapeDtypeStruct((rows, 1024), jnp.bfloat16),
        compiler_params=params(24),
        cost_estimate=cost(
            4 * rows * D * 1024,
            2 * D * (rows + 2048),
            rows * 1024,
        ),
        name="expert_in",
    )(*blocks, *gates, *ups, *after)


def expert_out_kernel(count, hidden, down_own, down_other, *refs):
    outs = refs[-count:]
    rows = outs[0].shape[0]
    for column in range(0, D, 512):
        cols = slice(column, column + 512)
        product = jnp.dot(
            hidden[:, :512], down_own[:, cols], preferred_element_type=jnp.float32
        ) + jnp.dot(hidden[:, 512:], down_other[:, cols], preferred_element_type=jnp.float32)
        for number, out in enumerate(outs):
            out[:, cols] = product[number * rows : (number + 1) * rows, :].astype(jnp.bfloat16)


def expert_out(hidden, downs, count, after=()):
    rows = hidden.shape[0]
    return pl.pallas_call(
        lambda *refs: expert_out_kernel(count, *refs),
        in_specs=[VMEM] * 3 + [ANY] * len(after),
        out_specs=[VMEM] * count,
        out_shape=[jax.ShapeDtypeStruct((rows // count, D), jnp.bfloat16)] * count,
        compiler_params=params(20),
        cost_estimate=cost(
            2 * rows * D * 1024,
            2 * D * (rows + 1024) + 2048 * rows,
            0,
        ),
        name="expert_out",
    )(hidden, *downs, *after)


def slot_table(ids_block, expert_count):
    flat_ids = ids_block.reshape(-1)
    onehot = (flat_ids[:, None] == jnp.arange(expert_count)[None, :]).astype(jnp.int32)
    earlier = jnp.cumsum(onehot, axis=0) - onehot
    return jnp.sum(earlier * onehot, axis=1)


def rope_tables():
    positions = np.arange(1024, dtype=np.float64)
    inverse = ROPE_BASE ** (-2.0 * np.arange(HD // 2) / HD)
    angles = np.repeat(positions[:, None] * inverse[None, :], 2, axis=1)
    sign = np.where(np.arange(HD) % 2 == 0, -1.0, 1.0)
    cosine = np.cos(angles).astype(np.float32).reshape(16, 64, HD)
    sine = (np.sin(angles) * sign).astype(np.float32).reshape(16, 64, HD)
    return cosine, sine


def on_device(
    tokens,
    attn_gain,
    query_weight,
    key_weight,
    value_weight,
    output_weight,
    ffn_gain,
    expert_gate,
    expert_up,
    expert_down,
    expert_ids,
    route_weights,
):
    expert_count = lax.axis_size("expert")
    rank = lax.axis_index("mp")
    core = rank % 2
    first = core == 0
    tok_rows = tokens.shape[0]
    inputs = tokens.astype(jnp.float32)
    normed = rms_norm(inputs, attn_gain).astype(jnp.bfloat16)

    blocks = gather_lane(normed)
    blocks.append(gather_last(blocks[4]))
    kv_own = jnp.concatenate([key_weight, value_weight], axis=1)
    kv_other = swap_cores(kv_own)
    query_other = swap_cores(query_weight)
    output_other = swap_cores(output_weight)
    places = jnp.stack(
        [
            jnp.where(
                first,
                *((rank // 4 + dx) % 4 * 4 + (rank // 2 % 2 ^ dz) * 2 for dx, dz in pair),
            )
            for pair in zip(*LABELS)
        ]
    )
    other_places = jnp.stack(
        [
            jnp.where(
                first,
                *((rank // 4 + dx) % 4 * 4 + (rank // 2 % 2 ^ dz) * 2 for dx, dz in pair[::-1]),
            )
            for pair in zip(*LABELS)
        ]
    )
    tables = [jnp.asarray(table) for table in rope_tables()]
    own_places = (places + core).astype(jnp.int32)
    offsets = jnp.arange(tok_rows)
    bases = own_places * tok_rows
    pos_own = (bases[:, None] + offsets[None, :]).reshape(-1)
    pos_other = ((other_places + 1 - core)[:, None] * tok_rows + offsets[None, :]).reshape(-1)
    weights = (query_weight, query_other, kv_own, kv_other)
    qkv_a = project(blocks[:4], weights, own_places[:4], *tables)
    qkv_b = project(blocks[4:], weights, own_places[4:], *tables, [qkv_a])
    kv_lane = jnp.concatenate([qkv_a[:, 512:], qkv_b[:, 512:]], axis=0)
    other = swap_cores(kv_lane)
    parts = attend(
        bases,
        qkv_a,
        qkv_b,
        other,
        jnp.concatenate([pos_own, pos_other]).astype(jnp.int32)[None, :],
        output_weight,
        output_other,
    )
    attn_sum = scatter_lane(parts, swapped=True)
    attended = (inputs + attn_sum).astype(jnp.bfloat16)
    normed_ffn = rms_norm(attended.astype(jnp.float32), ffn_gain).astype(jnp.bfloat16)

    capacity = 3 * tok_rows // expert_count
    slot_count = expert_count * capacity
    slots = slot_table(expert_ids, expert_count)
    targets = expert_ids.reshape(-1) * capacity + slots
    matches = (targets[:, None] == jnp.arange(slot_count)[None, :]).astype(jnp.bfloat16)
    matches = matches.reshape(tok_rows, 2, slot_count)
    dispatch_map = matches[:, 0] + matches[:, 1]

    def exchange(value, width):
        value = value.reshape(expert_count, width, D)
        value = lax.all_to_all(value, "expert", split_axis=0, concat_axis=0, tiled=True)
        return value.reshape(expert_count * width, D)

    def take_slots(value, span):
        shape = value.shape[:-1]
        value = value.reshape(*shape, expert_count, capacity)[..., span]
        return value.reshape(*shape, -1)

    spans = (slice(0, 16), slice(16, 24))

    def dispatch(span):
        return jnp.einsum(
            "tc,td->cd",
            take_slots(dispatch_map, span),
            normed_ffn,
            preferred_element_type=jnp.float32,
        ).astype(jnp.bfloat16)

    def collect(span, summed):
        picked = jnp.einsum(
            "tkc,cd->tkd",
            take_slots(matches, span),
            exchange(summed.astype(jnp.bfloat16), span.stop - span.start),
            preferred_element_type=jnp.float32,
        )
        return jnp.sum(picked * route_weights[:, :, None], axis=1)

    incoming_p = exchange(dispatch(spans[0]), 16)
    incoming_q = exchange(tie(dispatch(spans[1]), incoming_p), 8)
    gate, up, down = expert_gate[0], expert_up[0], expert_down[0]
    staged = stage(
        (gate, up, down, swap_cores(gate), swap_cores(up), swap_cores(down)), [incoming_q]
    )
    gates, ups, downs = staged[0:6:3], staged[1:6:3], staged[2:6:3]
    incoming_q = tie(incoming_q, staged[6])
    rows_p = gather_lane(incoming_p)
    rows_q = gather_lane(incoming_q, True)
    hidden_pa = expert_in(rows_p[:4], gates, ups)
    parts_p = expert_out(hidden_pa, downs, 4)
    rows_p[4] = tie(rows_p[4], parts_p[0])
    rows_p.append(gather_last(rows_p[4]))
    hidden_qa = expert_in(rows_q[:4], gates, ups, [parts_p[0]])
    hidden_pb = expert_in(rows_p[4:7], gates, ups, [hidden_qa])
    parts_p += expert_out(hidden_pb, downs, 3)
    rows_q[4] = tie(rows_q[4], hidden_pb)
    rows_q.append(gather_last(rows_q[4], True))
    hidden_qb = expert_in(rows_q[4:7], gates, ups, [parts_p[-1]])
    parts_qb = expert_out(hidden_qb, downs, 3)
    parts_q = expert_out(hidden_qa, downs, 4, [parts_qb[0]])
    parts_p += expert_out(expert_in(rows_p[7:], gates, ups, [parts_q[0]]), downs, 1)
    parts_q += parts_qb
    parts_q += expert_out(expert_in(rows_q[7:], gates, ups, [parts_p[-1]]), downs, 1)
    total = collect(spans[0], scatter_lane(parts_p))
    total += collect(spans[1], scatter_lane(parts_q, True))
    expert_mix = total.astype(jnp.bfloat16)
    return (attended, expert_mix)


def solution(mesh):
    in_specs = (
        P(("expert", "mp"), None),
        P(),
        P(None, "mp"),
        P(None, "mp"),
        P(None, "mp"),
        P("mp", None),
        P(),
        P("expert", None, "mp"),
        P("expert", None, "mp"),
        P("expert", "mp", None),
        P(("expert", "mp"), None),
        P(("expert", "mp"), None),
    )
    out_specs = (P(("expert", "mp"), None), P(("expert", "mp"), None))
    return jax.shard_map(
        on_device, mesh=mesh, in_specs=in_specs, out_specs=out_specs, check_vma=False
    )
```

```python
import math

import jax
import jax.numpy as jnp
import numpy as np
from jax import lax
from jax.experimental import pallas as pl
from jax.experimental.pallas import tpu as pltpu
from jax.sharding import PartitionSpec as P

D = 4096
HD = 128
EPSILON = 1e-05
ROPE_BASE = 1000000.0
SHARE = 0.4
LABELS = (
    ((0, 0), (0, 1), (-1, 0), (1, 0), (1, 1), (-1, 1), (2, 0), (2, 1)),
    ((0, 0), (-1, 0), (0, 1), (1, 0), (2, 0), (-1, 1), (1, 1), (2, 1)),
)


def to_z(i):
    return i ^ 2


def to_right(i):
    return (i + 4) % 16


def to_left(i):
    return (i + 12) % 16


def to_core(i):
    return i ^ 1


def send(value, lane0, lane1):
    pairs = [(i, lane1(i) if i % 2 else lane0(i)) for i in range(16)]
    return lax.ppermute(value, "mp", pairs)


def swap_cores(value):
    return send(value, to_core, to_core)


def sides(mirrored):
    return (to_right, to_left) if mirrored else (to_left, to_right)


def gather_lane(own, mirrored=False):
    left, right = sides(mirrored)
    a = send(own, to_z, right)
    c = send(own, left, left)
    b = send(own, right, to_z)
    s = send(a, left, right)
    r5 = send(a, right, to_z)
    s1 = send(c, left, to_z)
    return [own, a, b, c, s, r5, s1]


def gather_last(s, mirrored=False):
    left, _ = sides(mirrored)
    return send(s, left, to_z)


def tie(value, *others):
    return pl.pallas_call(
        lambda *refs: None,
        in_specs=[ANY] * (1 + len(others)),
        out_specs=ANY,
        out_shape=jax.ShapeDtypeStruct(value.shape, value.dtype),
        input_output_aliases={0: 0},
        compiler_params=params(1),
        cost_estimate=cost(0, 0),
        name="tie",
    )(value, *others)


def add(base, *terms):
    total = base.astype(jnp.float32)
    for term in terms:
        total = total + term.astype(jnp.float32)
    return total


def scatter_lane(parts, mirrored=False, early=False, waits=((), ())):
    own, a, b, c, s, r5, s1, r7 = parts
    left, right = sides(mirrored)
    low = lambda value: value.astype(jnp.bfloat16)
    b_in = send(b, left, to_z)
    r5_in = send(r5, left, to_z)
    s1_in = send(s1, right, to_z)
    c_in = send(low(add(c, s1_in)), right, right)
    r7_in = send(r7, right, to_z)
    if early:
        r7_in = tie(r7_in, r5_in, s1_in)
    if waits[0]:
        r7_in = tie(r7_in, *waits[0])
    s_in = send(low(add(s, r7_in)), right, left)
    if waits[1]:
        s_in = tie(s_in, *waits[1])
    a_in = send(low(add(a, s_in, r5_in)), to_z, left)
    return add(own, b_in, c_in, a_in)


def rms_norm(inputs, gain):
    mean_square = jnp.mean(inputs * inputs, axis=-1, keepdims=True)
    return inputs * lax.rsqrt(mean_square + EPSILON) * gain


def cost(flops, bytes_accessed, transcendentals=0):
    return pl.CostEstimate(
        flops=int(SHARE * flops),
        bytes_accessed=int(SHARE * bytes_accessed),
        transcendentals=int(SHARE * transcendentals),
    )


def params(mebibytes):
    return pltpu.CompilerParams(vmem_limit_bytes=mebibytes * 1024 * 1024)


ANY = pl.BlockSpec(memory_space=pl.ANY)
SMEM = pl.BlockSpec(memory_space=pltpu.SMEM)
VMEM = pl.BlockSpec(memory_space=pltpu.VMEM)
HBM = pl.BlockSpec(memory_space=pltpu.HBM)


def stack(refs):
    return jnp.concatenate([ref[...] for ref in refs], axis=0)


def stage_kernel(*refs):
    count = len(refs) // 2
    sems = refs[-1]
    copies = [
        pltpu.make_async_copy(refs[number], refs[count + number], sems.at[number])
        for number in range(count)
    ]
    for copy in copies:
        copy.start()
    for copy in copies:
        copy.wait()


def stage(*arrays):
    return pl.pallas_call(
        stage_kernel,
        in_specs=[HBM] * len(arrays),
        out_specs=[VMEM] * len(arrays),
        out_shape=[jax.ShapeDtypeStruct(array.shape, array.dtype) for array in arrays],
        scratch_shapes=[pltpu.SemaphoreType.DMA((len(arrays),))],
        compiler_params=params(16),
        cost_estimate=cost(0, 2 * sum(array.size for array in arrays)),
        name="stage",
    )(*arrays)


def project_kernel(count, places, *refs):
    blocks, weights, tables = refs[:count], refs[count : count + 4], refs[count + 4 : count + 6]
    out = refs[-1]
    rows = out.shape[0]
    cosine, sine = (
        jnp.concatenate([table[places[number]] for number in range(count)], axis=0)
        for table in tables
    )
    lane = lax.broadcasted_iota(jnp.int32, (rows, HD), 1)

    def turn(head):
        swapped = jnp.where(lane % 2 == 0, pltpu.roll(head, HD - 1, 1), pltpu.roll(head, 1, 1))
        return (head * cosine + swapped * sine).astype(jnp.bfloat16)

    for number in range(2):
        product = jnp.dot(stack(blocks), weights[number][...], preferred_element_type=jnp.float32)
        for part in range(2):
            at = number * 256 + part * HD
            out[:, at : at + HD] = turn(product[:, part * HD : (part + 1) * HD])
    pair = jnp.concatenate([weights[2][...], weights[3][...]], axis=1)
    product = jnp.dot(stack(blocks), pair, preferred_element_type=jnp.float32)
    own, other = product[:, :HD], product[:, HD:]
    first = places[0] % 2 == 0
    low = jnp.where(first, own, other)
    high = jnp.where(first, other, own)
    below = lane < HD // 2
    out[:, 512:640] = turn(jnp.where(below, low, pltpu.roll(high, HD // 2, 1)))
    out[:, 640:768] = jnp.where(below, pltpu.roll(low, HD // 2, 1), high).astype(jnp.bfloat16)


def project(blocks, weights, places, cosine, sine):
    count = len(blocks)
    rows = sum(block.shape[0] for block in blocks)
    return pl.pallas_call(
        lambda *refs: project_kernel(count, *refs),
        in_specs=[SMEM] + [VMEM] * (count + 6),
        out_specs=VMEM,
        out_shape=jax.ShapeDtypeStruct((rows, 768), jnp.bfloat16),
        compiler_params=params(20),
        cost_estimate=cost(
            2 * rows * D * 768, 2 * D * (rows + 768), 0
        ),
        name="project",
    )(places, *blocks, *weights, cosine, sine)


def attend_kernel(bases, qkv_a, qkv_b, other, pos_k, out_own, out_other, *refs):
    outs = refs[:8]
    keys, values, scores, weights, context, result, out_sems = refs[8:]
    half = qkv_a.shape[0]
    rows = 2 * half
    block = outs[0].shape[0]
    for number, source in enumerate((qkv_a, qkv_b)):
        span = slice(number * half, (number + 1) * half)
        keys[span, :] = source[:, 512:640]
        values[span, :] = source[:, 640:768]
    keys[rows:, :] = other[:, :HD]
    values[rows:, :] = other[:, HD:]
    scale = math.log2(math.e) / math.sqrt(HD)
    tiles = rows // 128
    out_copies = []
    for tile in range(tiles):
        slot = tile % 2
        source = (qkv_a, qkv_b)[tile * 128 // half]
        at = tile * 128 % half
        queries = jnp.concatenate(
            [source[at : at + 128, head * HD : (head + 1) * HD] for head in range(4)], axis=0
        )
        scores[slot] = lax.dot_general(
            queries, keys[...], (((1,), (1,)), ((), ())), preferred_element_type=jnp.float32
        )
        sums = []
        for piece in range(8):
            start = piece * 64
            pos_q = bases[2 * tile + piece % 2] + lax.broadcasted_iota(jnp.int32, (64, 1), 0)
            masked = jnp.where(pos_q >= pos_k[...], scores[slot, start : start + 64, :], -1e30)
            maxima = jnp.max(masked, axis=-1, keepdims=True)
            expo = jnp.exp2(masked * scale - maxima * scale)
            sums.append(jnp.sum(expo, axis=-1, keepdims=True))
            weights[slot, start : start + 64, :] = expo.astype(jnp.bfloat16)
        mixed = jnp.dot(weights[slot], values[...], preferred_element_type=jnp.float32)
        mixed = (mixed / jnp.concatenate(sums, axis=0)).astype(jnp.bfloat16)
        for head in range(4):
            context[tile * 128 : (tile + 1) * 128, head * HD : (head + 1) * HD] = mixed[
                head * 128 : (head + 1) * 128, :
            ]
        if tile % 2:
            pair = slice((tile - 1) * 128, (tile + 1) * 128)
            for column in range(0, D, 1024):
                cols = slice(column, column + 1024)
                product = jnp.dot(
                    context[pair, :256], out_own[:, cols], preferred_element_type=jnp.float32
                ) + jnp.dot(
                    context[pair, 256:], out_other[:, cols], preferred_element_type=jnp.float32
                )
                result[pair, cols] = product.astype(jnp.bfloat16)
            for number in range((tile - 1) * 128 // block, (tile + 1) * 128 // block):
                copy = pltpu.make_async_copy(
                    result.at[pl.ds(number * block, block), :], outs[number], out_sems.at[number]
                )
                copy.start()
                out_copies.append(copy)
    for copy in out_copies:
        copy.wait()


def attend(bases, qkv_a, qkv_b, other, pos_k, out_own, out_other):
    rows = qkv_a.shape[0] + qkv_b.shape[0]
    block = rows // 8
    operands = (qkv_a, qkv_b, other, pos_k)
    return pl.pallas_call(
        attend_kernel,
        in_specs=[SMEM] + [VMEM] * 6,
        out_specs=[ANY] * 8,
        out_shape=[jax.ShapeDtypeStruct((block, D), jnp.bfloat16)] * 8,
        scratch_shapes=[
            pltpu.VMEM((2 * rows, HD), jnp.bfloat16),
            pltpu.VMEM((2 * rows, HD), jnp.bfloat16),
            pltpu.VMEM((2, 512, 2 * rows), jnp.float32),
            pltpu.VMEM((2, 512, 2 * rows), jnp.bfloat16),
            pltpu.VMEM((rows, 512), jnp.bfloat16),
            pltpu.VMEM((rows, D), jnp.bfloat16),
            pltpu.SemaphoreType.DMA((8,)),
        ],
        compiler_params=params(28),
        cost_estimate=cost(
            4 * rows * 512 * rows * 2 + 2 * rows * 512 * D,
            16 * 1024 * 1024,
            4 * rows * rows * 2,
        ),
        name="attend",
    )(bases, *operands, out_own, out_other)


def expert_in_kernel(count, *refs):
    blocks, weights, out = refs[:count], refs[count : count + 4], refs[-1]
    for part in range(2):
        for column in (0, 256):
            cols = slice(column, column + 256)
            gate = jnp.dot(stack(blocks), weights[part][:, cols], preferred_element_type=jnp.float32)
            up = jnp.dot(
                stack(blocks), weights[2 + part][:, cols], preferred_element_type=jnp.float32
            )
            hidden = gate / (1.0 + jnp.exp(-gate)) * up
            at = part * 512 + column
            out[:, at : at + 256] = hidden.astype(jnp.bfloat16)


def expert_in(blocks, gates, ups, after=()):
    rows = sum(block.shape[0] for block in blocks)
    return pl.pallas_call(
        lambda *refs: expert_in_kernel(len(blocks), *refs),
        in_specs=[VMEM] * (len(blocks) + 4) + [ANY] * len(after),
        out_specs=VMEM,
        out_shape=jax.ShapeDtypeStruct((rows, 1024), jnp.bfloat16),
        compiler_params=params(24),
        cost_estimate=cost(
            4 * rows * D * 1024,
            2 * D * (rows + 2048),
            rows * 1024,
        ),
        name="expert_in",
    )(*blocks, *gates, *ups, *after)


def expert_out_kernel(count, hidden, down_own, down_other, *refs):
    outs = refs[-count:]
    rows = outs[0].shape[0]
    for column in range(0, D, 512):
        cols = slice(column, column + 512)
        product = jnp.dot(
            hidden[:, :512], down_own[:, cols], preferred_element_type=jnp.float32
        ) + jnp.dot(hidden[:, 512:], down_other[:, cols], preferred_element_type=jnp.float32)
        for number, out in enumerate(outs):
            out[:, cols] = product[number * rows : (number + 1) * rows, :].astype(jnp.bfloat16)


def expert_out(hidden, downs, count, after=()):
    rows = hidden.shape[0]
    return pl.pallas_call(
        lambda *refs: expert_out_kernel(count, *refs),
        in_specs=[VMEM] * 3 + [ANY] * len(after),
        out_specs=[VMEM] * count,
        out_shape=[jax.ShapeDtypeStruct((rows // count, D), jnp.bfloat16)] * count,
        compiler_params=params(20),
        cost_estimate=cost(
            2 * rows * D * 1024,
            2 * D * (rows + 1024) + 2048 * rows,
            0,
        ),
        name="expert_out",
    )(hidden, *downs, *after)


def slot_table(ids_block, expert_count):
    flat_ids = ids_block.reshape(-1)
    onehot = (flat_ids[:, None] == jnp.arange(expert_count)[None, :]).astype(jnp.int32)
    earlier = jnp.cumsum(onehot, axis=0) - onehot
    return jnp.sum(earlier * onehot, axis=1)


def rope_tables():
    positions = np.arange(1024, dtype=np.float64)
    inverse = ROPE_BASE ** (-2.0 * np.arange(HD // 2) / HD)
    angles = np.repeat(positions[:, None] * inverse[None, :], 2, axis=1)
    sign = np.where(np.arange(HD) % 2 == 0, -1.0, 1.0)
    cosine = np.cos(angles).astype(np.float32).reshape(16, 64, HD)
    sine = (np.sin(angles) * sign).astype(np.float32).reshape(16, 64, HD)
    return cosine, sine


def on_device(
    tokens,
    attn_gain,
    query_weight,
    key_weight,
    value_weight,
    output_weight,
    ffn_gain,
    expert_gate,
    expert_up,
    expert_down,
    expert_ids,
    route_weights,
):
    expert_count = lax.axis_size("expert")
    rank = lax.axis_index("mp")
    core = rank % 2
    first = core == 0
    tok_rows = tokens.shape[0]
    inputs = tokens.astype(jnp.float32)
    normed = rms_norm(inputs, attn_gain).astype(jnp.bfloat16)

    blocks = gather_lane(normed)
    blocks.append(gather_last(blocks[4]))
    kv_own = jnp.concatenate([key_weight, value_weight], axis=1)
    kv_other = swap_cores(kv_own)
    query_other = swap_cores(query_weight)
    output_other = swap_cores(output_weight)
    places = jnp.stack(
        [
            jnp.where(
                first,
                *((rank // 4 + dx) % 4 * 4 + (rank // 2 % 2 ^ dz) * 2 for dx, dz in pair),
            )
            for pair in zip(*LABELS)
        ]
    )
    other_places = jnp.stack(
        [
            jnp.where(
                first,
                *((rank // 4 + dx) % 4 * 4 + (rank // 2 % 2 ^ dz) * 2 for dx, dz in pair[::-1]),
            )
            for pair in zip(*LABELS)
        ]
    )
    tables = [jnp.asarray(table) for table in rope_tables()]
    own_places = (places + core).astype(jnp.int32)
    offsets = jnp.arange(tok_rows)
    bases = own_places * tok_rows
    pos_own = (bases[:, None] + offsets[None, :]).reshape(-1)
    pos_other = ((other_places + 1 - core)[:, None] * tok_rows + offsets[None, :]).reshape(-1)
    weights = (query_weight, query_other, kv_own, kv_other)
    qkv_a = project(blocks[:4], weights, own_places[:4], *tables)
    gate_own, up_own, down_own = expert_gate[0], expert_up[0], expert_down[0]
    others = stage(swap_cores(gate_own), swap_cores(up_own), swap_cores(down_own))
    owns = stage(gate_own, up_own, down_own)
    gates, ups, downs = zip(owns, others)
    qkv_b = project(blocks[4:], weights, own_places[4:], *tables)
    kv_lane = jnp.concatenate([qkv_a[:, 512:], qkv_b[:, 512:]], axis=0)
    other = swap_cores(kv_lane)
    parts = attend(
        bases,
        qkv_a,
        qkv_b,
        other,
        jnp.concatenate([pos_own, pos_other]).astype(jnp.int32)[None, :],
        output_weight,
        output_other,
    )
    attn_sum = scatter_lane(parts, waits=(owns, others))
    attended = (inputs + attn_sum).astype(jnp.bfloat16)
    normed_ffn = rms_norm(attended.astype(jnp.float32), ffn_gain).astype(jnp.bfloat16)

    capacity = 3 * tok_rows // expert_count
    slot_count = expert_count * capacity
    slots = slot_table(expert_ids, expert_count)
    targets = expert_ids.reshape(-1) * capacity + slots
    matches = (targets[:, None] == jnp.arange(slot_count)[None, :]).astype(jnp.bfloat16)
    matches = matches.reshape(tok_rows, 2, slot_count)
    dispatch_map = matches[:, 0] + matches[:, 1]

    def exchange(value, width):
        value = value.reshape(expert_count, width, D)
        value = lax.all_to_all(value, "expert", split_axis=0, concat_axis=0, tiled=True)
        return value.reshape(expert_count * width, D)

    def take_slots(value, span):
        shape = value.shape[:-1]
        value = value.reshape(*shape, expert_count, capacity)[..., span]
        return value.reshape(*shape, -1)

    spans = (slice(0, 16), slice(16, 24))

    def dispatch(span):
        return jnp.einsum(
            "tc,td->cd",
            take_slots(dispatch_map, span),
            normed_ffn,
            preferred_element_type=jnp.float32,
        ).astype(jnp.bfloat16)

    def collect(span, summed):
        picked = jnp.einsum(
            "tkc,cd->tkd",
            take_slots(matches, span),
            exchange(summed.astype(jnp.bfloat16), span.stop - span.start),
            preferred_element_type=jnp.float32,
        )
        return jnp.sum(picked * route_weights[:, :, None], axis=1)

    incoming_p = exchange(dispatch(spans[0]), 16)
    incoming_q = exchange(tie(dispatch(spans[1]), incoming_p), 8)
    rows_p = gather_lane(incoming_p)
    rows_q = gather_lane(incoming_q, True)
    hidden_pa = expert_in(rows_p[:4], gates, ups, [incoming_q])
    parts_p = expert_out(hidden_pa, downs, 4)
    rows_p[4] = tie(rows_p[4], parts_p[0])
    rows_p.append(gather_last(rows_p[4]))
    hidden_qa = expert_in(rows_q[:4], gates, ups, [parts_p[0]])
    hidden_pb = expert_in(rows_p[4:7], gates, ups, [hidden_qa])
    parts_p += expert_out(hidden_pb, downs, 3)
    rows_q[4] = tie(rows_q[4], hidden_pb)
    rows_q.append(gather_last(rows_q[4], True))
    hidden_qb = expert_in(rows_q[4:7], gates, ups, [parts_p[-1]])
    parts_qb = expert_out(hidden_qb, downs, 3)
    parts_q = expert_out(hidden_qa, downs, 4, [parts_qb[0]])
    parts_p += expert_out(expert_in(rows_p[7:], gates, ups, [parts_q[0]]), downs, 1)
    parts_q += parts_qb
    parts_q += expert_out(expert_in(rows_q[7:], gates, ups, [parts_p[-1]]), downs, 1)
    total = collect(spans[0], scatter_lane(parts_p, False, True))
    total += collect(spans[1], scatter_lane(parts_q, True, True))
    expert_mix = total.astype(jnp.bfloat16)
    return (attended, expert_mix)


def solution(mesh):
    in_specs = (
        P(("expert", "mp"), None),
        P(),
        P(None, "mp"),
        P(None, "mp"),
        P(None, "mp"),
        P("mp", None),
        P(),
        P("expert", None, "mp"),
        P("expert", None, "mp"),
        P("expert", "mp", None),
        P(("expert", "mp"), None),
        P(("expert", "mp"), None),
    )
    out_specs = (P(("expert", "mp"), None), P(("expert", "mp"), None))
    return jax.shard_map(
        on_device, mesh=mesh, in_specs=in_specs, out_specs=out_specs, check_vma=False
    )
```
